128 devices in a mesh: ep: 32 (over z, y_lo, x), rep: 4 (over y_hi, core).
Axes of the slice: x: 4, y: 4 (y_hi: 2, y_lo: 2; y = y_hi * 2 + y_lo), z: 4, core: 2. Of those that a mesh axis runs over, the one named last changes fastest.
Arguments:
- tokens: bfloat16 [16384, 4096], P(('ep', 'rep')), may hold values from -6 to 6
- expert_ids: int32 [16384, 2], P(('ep', 'rep')), may hold values from 0 to 63, as said below
- route_weights: float32 [16384, 2], P(('ep', 'rep')), may hold values from 0.1 to 1
- w_gate: bfloat16 [4, 4096, 8192], P('rep', None, 'ep'), may hold values from -0.09375 to 0.09375
- w_up: bfloat16 [4, 4096, 8192], P('rep', None, 'ep'), may hold values from -0.09375 to 0.09375
- w_down: bfloat16 [4, 8192, 4096], P('rep', 'ep'), may hold values from -0.0625 to 0.0625
- cotangent: bfloat16 [16384, 4096], P(('ep', 'rep')), may hold values from -6 to 6
Outputs:
- mixed: bfloat16 [16384, 4096], P(('ep', 'rep'))
- grad_tokens: bfloat16 [16384, 4096], P(('ep', 'rep'))
- grad_gate: bfloat16 [4, 4096, 8192], P('rep', None, 'ep')
- grad_up: bfloat16 [4, 4096, 8192], P('rep', None, 'ep')
- grad_down: bfloat16 [4, 8192, 4096], P('rep', 'ep')
The draws below stay inside these ranges and needn't reach their ends.
Inputs may be any that keep to these rules, and one draw needn't show every extreme that they name: `expert_ids`: A token's two experts differ. Among the rows of one device, each expert below 4 is named at most 4 times; one of them is named exactly 4 times by every device.
All inputs are finite; a program needn't handle non-finite values.
Results may differ from the reference program's by a relative error of at most 0.0058.
Values may be sent and summed in bfloat16 or wider, within the bound.
A program may use at most 128 MiB of HBM per device.

```python
import jax
import jax.numpy as jnp
from jax import lax

D = 4096
EXPERTS_ALL = 64
TOK_DEV = 128
CAP = 4
FF = 8192
WIN = 4
TOKENS = 16384
DEVICES = 128


def draw_expert_ids(key, part):
    favored = jax.random.randint(jax.random.fold_in(key, 3), (), 0, WIN)
    outside = EXPERTS_ALL - WIN

    def one_block(index):
        block_key = jax.random.fold_in(jax.random.fold_in(key, 11), index)
        counts = jax.random.randint(jax.random.fold_in(block_key, 1), (WIN,), 1, CAP + 1)
        counts = jnp.where(jnp.arange(WIN, dtype=jnp.int32) == favored, CAP, counts)
        lanes = jnp.arange(WIN * CAP, dtype=jnp.int32)
        which = lanes // CAP
        valid = lanes % CAP < counts[which]
        chosen = jax.random.permutation(jax.random.fold_in(block_key, 2), TOK_DEV)[:WIN * CAP]
        inside = jnp.full((TOK_DEV,), -1, jnp.int32).at[chosen].set(jnp.where(valid, which, -1).astype(jnp.int32))
        first = jax.random.randint(jax.random.fold_in(block_key, 3), (TOK_DEV,), 0, outside)
        offset = jax.random.randint(jax.random.fold_in(block_key, 4), (TOK_DEV,), 1, outside)
        second = (first + offset) % outside
        column = jax.random.randint(jax.random.fold_in(block_key, 5), (TOK_DEV,), 0, 2)
        left = jnp.where((inside >= 0) & (column == 0), inside, first + WIN)
        right = jnp.where((inside >= 0) & (column == 1), inside, second + WIN)
        return jnp.stack([left, right], axis=1).astype(jnp.int32)
    return lax.map(one_block, jnp.arange(DEVICES, dtype=jnp.int32)).reshape(TOKENS, 2)


def steps_of(key, extent, cuts, low, top_value):
    factor_of, own = 1.0, jax.random.fold_in(key, 6)
    for dim, blocks in cuts:
        steps = jnp.exp(jax.random.uniform(jax.random.fold_in(own, dim), (blocks,), jnp.float32, low / len(cuts), top_value / len(cuts)))
        factor_of = factor_of * jnp.repeat(steps, extent[dim] // blocks).reshape([-1 if axis == dim else 1 for axis in range(len(extent))])
    return factor_of


def scatter_about(rng, extent, spread, limit, shards=(), held_as=jnp.bfloat16):
    level = steps_of(rng, extent, shards, -0.22, 0.18) if shards else 1.0
    result = jax.random.normal(rng, extent, jnp.float32) * spread * level
    return jnp.minimum(jnp.maximum(result, -limit), limit).astype(held_as)


def setup_inputs(seed: int = 0) -> dict:
    streams_of = jax.random.split(jax.random.key(seed), 8)
    return {
        "tokens": scatter_about(streams_of[0], (TOKENS, D), 1.0, 6.0, ((0, 128),)),
        "expert_ids": draw_expert_ids(jax.random.fold_in(streams_of[7], 71), 0),
        "route_weights": jnp.clip(0.1 + 0.9 * jax.random.uniform(streams_of[2], (TOKENS, 2), jnp.float32) ** steps_of(streams_of[2], (TOKENS, 2), ((0, 128),), -0.2, 0.2), 0.1, 1.0),
        "w_gate": scatter_about(streams_of[3], (WIN, D, FF), D ** -0.5, 0.09375, ((0, 4), (2, 32))),
        "w_up": scatter_about(streams_of[4], (WIN, D, FF), D ** -0.5, 0.09375, ((0, 4), (2, 32))),
        "w_down": scatter_about(streams_of[5], (WIN, FF, D), FF ** -0.5, 0.0625, ((0, 4), (1, 32))),
        "cotangent": scatter_about(streams_of[6], (TOKENS, D), 1.0, 6.0, ((0, 128),)),
    }


def reference(tokens, expert_ids, route_weights, w_gate, w_up, w_down, cotangent):
    routes = TOKENS * 2
    most = DEVICES * CAP
    flat_e = expert_ids.reshape(-1)
    bucket = jnp.minimum(flat_e, WIN).astype(jnp.int32)
    order = jnp.argsort(bucket, stable=True).astype(jnp.int32)
    counts = jax.ops.segment_sum(jnp.ones((routes,), jnp.int32), bucket, num_segments=WIN + 1)
    starts = (jnp.cumsum(counts) - counts).astype(jnp.int32)
    order_pad = jnp.concatenate([order, jnp.zeros((most,), jnp.int32)])
    flat_weights = route_weights.reshape(-1)
    lanes = jnp.arange(most, dtype=jnp.int32)

    def per_expert(carry, inputs):
        mixed_acc, grad_acc = carry
        wg, wu, wd, expert = inputs
        picked = lax.dynamic_slice(order_pad, (starts[expert].astype(jnp.int32),), (most,))
        valid = lanes < counts[expert]
        token_of = picked // 2
        weight = jnp.where(valid, flat_weights[picked], 0.0)
        rows = jnp.where(valid[:, None], tokens[token_of], jnp.zeros((), jnp.bfloat16))
        pre_gate = jnp.dot(rows, wg, preferred_element_type=jnp.float32)
        pre_up = jnp.dot(rows, wu, preferred_element_type=jnp.float32)
        logistic = jax.nn.sigmoid(pre_gate)
        activated = pre_gate * logistic
        hidden = (activated * pre_up).astype(jnp.bfloat16)
        routed = jnp.dot(hidden, wd, preferred_element_type=jnp.float32).astype(jnp.bfloat16)
        mixed_acc = mixed_acc.at[token_of].add(weight[:, None] * routed.astype(jnp.float32))
        upstream = (weight[:, None] * cotangent[token_of].astype(jnp.float32)).astype(jnp.bfloat16)
        d_act = jnp.dot(upstream, wd.T, preferred_element_type=jnp.float32)
        d_up = (d_act * activated).astype(jnp.bfloat16)
        d_gate = (d_act * pre_up * logistic * (1.0 + pre_gate * (1.0 - logistic))).astype(jnp.bfloat16)
        grad_sum = jnp.dot(d_gate, wg.T, preferred_element_type=jnp.float32) + jnp.dot(d_up, wu.T, preferred_element_type=jnp.float32)
        route_grad = grad_sum.astype(jnp.bfloat16)
        grad_acc = grad_acc.at[token_of].add(jnp.where(valid[:, None], route_grad.astype(jnp.float32), 0.0))
        part_gate = jnp.dot(rows.T, d_gate, preferred_element_type=jnp.float32).astype(jnp.bfloat16)
        part_up = jnp.dot(rows.T, d_up, preferred_element_type=jnp.float32).astype(jnp.bfloat16)
        part_down = jnp.dot(hidden.T, upstream, preferred_element_type=jnp.float32).astype(jnp.bfloat16)
        return (mixed_acc, grad_acc), (part_gate, part_up, part_down)

    begin = (jnp.zeros((TOKENS, D), jnp.float32), jnp.zeros((TOKENS, D), jnp.float32))
    (mixed_acc, grad_acc), grads = lax.scan(per_expert, begin, (w_gate, w_up, w_down, jnp.arange(WIN, dtype=jnp.int32)))
    return mixed_acc.astype(jnp.bfloat16), grad_acc.astype(jnp.bfloat16), grads[0], grads[1], grads[2]
```

```python
import functools

import jax
import jax.numpy as jnp
from jax import lax
from jax.experimental import pallas as pl
from jax.experimental.pallas import tpu as pltpu
from jax.sharding import PartitionSpec as P

MESH = pl.DeviceIdType.MESH
F32, BF16 = jnp.float32, jnp.bfloat16
D, FF, TOK, SLOT = 4096, 256, 128, 16
QUARTER = D // 4
SIZES = {"z": 4, "y": 2, "x": 4}
PARTS = (
    (0, 1408, "yzx"),
    (1408, 2816, "yxz"),
    (2816, 3456, "zxy"),
    (3456, 4096, "xzy"),
)
COPIES = 200


def dot(a, b, ca=1, cb=0):
    return lax.dot_general(a, b, (((ca,), (cb,)), ((), ())), preferred_element_type=F32)


def stages(part):
    order = part[2]
    for s, axis in enumerate(order):
        free = order[:s]
        halved = "y" if "y" in free else (free[0] if free else None)
        yield axis, free, halved


def kernel(
    ids_ref, wts_ref, tok_hbm, cot_hbm, wg_hbm, wu_hbm, wd_hbm,
    mixed_hbm, gtok_hbm, gg_hbm, gu_hbm, gd_hbm,
    tok, cot, wg, wu, wd, xs, us, ps, qs, act, fac, hid, dgu, gg, gu, gd,
    out_m, out_g, box_s, box_r, local_sem, send_sem, recv_sem, *landing,
):
    ep, rep = lax.axis_index("ep"), lax.axis_index("rep")
    own = {"z": ep // 8, "y": (ep // 4) % 2, "x": ep % 4}
    half, core = rep // 2, rep % 2

    def place(z=None, y=None, x=None, h=None, c=None):
        z, y, x = (own[k] if v is None else v for k, v in (("z", z), ("y", y), ("x", x)))
        return (z * 8 + y * 4 + x, (half if h is None else h) * 2 + (core if c is None else c))

    after = {a: (own[a] + 1) % SIZES[a] for a in SIZES}
    before = {a: (own[a] + SIZES[a] - 1) % SIZES[a] for a in SIZES}
    far = {a: (own[a] + 2) % SIZES[a] for a in SIZES}

    def fetch(src, dst, i):
        copy = pltpu.make_async_copy(src, dst, local_sem.at[i])
        copy.start()
        return copy

    get_tok = fetch(tok_hbm, tok, 0)
    get_cot = fetch(cot_hbm, cot, 1)
    get_w = [fetch(wg_hbm.at[0], wg, 2), fetch(wu_hbm.at[0], wu, 3), fetch(wd_hbm.at[0], wd, 4)]

    traders = [place(c=1 - core), place(y=1 - own["y"], h=1 - half), place(y=1 - own["y"], h=1 - half, c=1 - core)]
    neighbours = traders + [place(y=1 - own["y"])]
    for a in "zx":
        neighbours += [place(**{a: after[a]}), place(**{a: before[a]})]
    barrier = pltpu.get_barrier_semaphore()
    for device in neighbours:
        pl.semaphore_signal(barrier, inc=1, device_id=device, device_id_type=MESH)

    sent = []

    def send(src, dst, device):
        i = len(sent)
        copy = pltpu.make_async_remote_copy(
            src, dst, send_sem.at[i], recv_sem.at[i], device_id=device, device_id_type=MESH
        )
        copy.start()
        sent.append(copy)
        return copy

    ids = ids_ref[...].astype(F32)
    wts = wts_ref[...]
    along = [jnp.broadcast_to(ids[:, k : k + 1], (TOK, TOK)).T[:64] for k in range(2)]
    w_along = [jnp.broadcast_to(wts[:, k : k + 1], (TOK, TOK)).T[:64] for k in range(2)]
    row = lax.broadcasted_iota(jnp.int32, (64, TOK), 0)
    expert, quarter, spot = row // 16, (row // 4) % 4, (row % 4).astype(F32)
    one = [jnp.where(a == expert.astype(F32), 1.0, 0.0).astype(F32) for a in along]
    hit = one[0] + one[1]
    t0 = lax.broadcasted_iota(jnp.int32, (TOK, TOK), 0)
    t1 = lax.broadcasted_iota(jnp.int32, (TOK, TOK), 1)
    earlier = dot(hit.astype(BF16), jnp.where(t0 < t1, 1.0, 0.0).astype(BF16))
    taken = jnp.where(earlier == spot, hit, 0.0)
    row_weight = jnp.sum(taken * (one[0] * w_along[0] + one[1] * w_along[1]), axis=1, keepdims=True)
    pick = [jnp.where(quarter == q, taken, 0.0).astype(BF16) for q in range(4)]

    def pack(values):
        return sum(dot(pick[q], values[:, q * QUARTER : (q + 1) * QUARTER]) for q in range(4))

    def trade(n):
        copies = [send(box_s.at[n, d[1]], box_r.at[n, rep], d) for d in traders]
        box_r[n, rep] = box_s[n, rep]
        return copies

    get_tok.wait()
    box_s[0] = pack(tok[...]).astype(BF16).reshape(4, 16, QUARTER)
    pl.semaphore_wait(barrier, len(neighbours))
    trade_x = trade(0)
    get_cot.wait()
    box_s[1] = (pack(cot[...]) * row_weight).astype(BF16).reshape(4, 16, QUARTER)
    trade_u = trade(1)

    def settle(copies, n, buf):
        for copy in copies:
            copy.wait_recv()
        r = lax.broadcasted_iota(jnp.int32, (16, 64), 0)
        s = lax.broadcasted_iota(jnp.int32, (16, 64), 1)
        blocks = box_r[n].reshape(64, QUARTER)
        for q in range(4):
            turn = jnp.where(s == (r // 4) * 16 + q * 4 + r % 4, 1.0, 0.0).astype(BF16)
            buf[own["z"], own["y"], own["x"], :, q * QUARTER : (q + 1) * QUARTER] = dot(turn, blocks).astype(BF16)

    def region(part, axis, at, free, halved, which=None):
        lo, hi, _ = part
        index = []
        for a in "zyx":
            if a == axis:
                index.append(pl.ds(at, 1))
            elif a in free:
                n = SIZES[a]
                if which is None or a != halved:
                    index.append(pl.ds(0, n))
                else:
                    index.append(pl.ds(which * (n // 2), n // 2))
            else:
                index.append(pl.ds(own[a], 1))
        if which is not None and halved is None:
            cut = lo + 384
            lo, hi = (lo, cut) if which == 0 else (cut, hi)
        return (*index, slice(None), pl.ds(lo, hi - lo))

    def within(part, free, halved, which):
        lo, hi, _ = part
        index = [
            pl.ds(which * (SIZES[a] // 2), SIZES[a] // 2) if a == halved else slice(None) for a in "zyx"
        ]
        cols = slice(None)
        if halved is None:
            cols = pl.ds(0, 384) if which == 0 else pl.ds(384, hi - lo - 384)
        return (*index, slice(None), cols)

    def gather(part, buf):
        for axis, free, halved in stages(part):
            mine = buf.at[region(part, axis, own[axis], free, halved)]
            up, down = place(**{axis: after[axis]}), place(**{axis: before[axis]})
            if SIZES[axis] == 2:
                copy = send(mine, mine, up)
                yield
                copy.wait_recv()
                continue
            a, b = send(mine, mine, up), send(mine, mine, down)
            yield
            a.wait_recv()
            r = buf.at[region(part, axis, before[axis], free, halved, 0)]
            a = send(r, r, up)
            b.wait_recv()
            r = buf.at[region(part, axis, after[axis], free, halved, 1)]
            b = send(r, r, down)
            yield
            a.wait_recv()
            b.wait_recv()

    landing = list(landing)

    def scatter(part, buf):
        shapes = landings(part)
        spare = iter(landing[: len(shapes)])
        del landing[: len(shapes)]
        return walk_back(part, buf, spare)

    def walk_back(part, buf, spare):
        for axis, free, halved in reversed(list(stages(part))):
            up, down = place(**{axis: after[axis]}), place(**{axis: before[axis]})
            mine = region(part, axis, own[axis], free, halved)
            if SIZES[axis] == 2:
                land = next(spare)
                copy = send(buf.at[region(part, axis, after[axis], free, halved)], land, up)
                yield
                copy.wait_recv()
                buf[mine] = (buf[mine].astype(F32) + land[...].astype(F32)).astype(BF16)
                continue
            via_l, via_r, land_l, land_r = next(spare), next(spare), next(spare), next(spare)
            half0, half1 = (within(part, free, halved, w) for w in (0, 1))
            o0 = send(buf.at[region(part, axis, far[axis], free, halved, 0)], via_l, up)
            o1 = send(buf.at[region(part, axis, far[axis], free, halved, 1)], via_r, down)
            e1 = send(buf.at[region(part, axis, after[axis], free, halved, 1)], land_l.at[half1], up)
            e0 = send(buf.at[region(part, axis, before[axis], free, halved, 0)], land_r.at[half0], down)
            yield
            o0.wait_recv()
            r = region(part, axis, after[axis], free, halved, 0)
            buf[r] = (buf[r].astype(F32) + via_l[...].astype(F32)).astype(BF16)
            f0 = send(buf.at[r], land_l.at[half0], up)
            o1.wait_recv()
            r = region(part, axis, before[axis], free, halved, 1)
            buf[r] = (buf[r].astype(F32) + via_r[...].astype(F32)).astype(BF16)
            f1 = send(buf.at[r], land_r.at[half1], down)
            yield
            for copy in (e1, e0, f0, f1):
                copy.wait_recv()
            buf[mine] = (buf[mine].astype(F32) + land_l[...].astype(F32) + land_r[...].astype(F32)).astype(BF16)

    def go(walks, which=(0, 1, 2, 3)):
        for w in which:
            next(walks[w], None)

    def rows(i):
        return pl.ds(pl.multiple_of(i * 256, 256), 256)

    def forward():
        @pl.loop(0, 2)
        def _(i):
            z = pl.ds(i * 2, 2)
            x = xs[z].reshape(256, D)
            g = dot(x, wg[...])
            u = dot(x, wu[...])
            s = 1.0 / (1.0 + jnp.exp(-g))
            a = g * s
            h = (a * u).astype(BF16)
            act[rows(i), :] = a
            fac[rows(i), :] = u * s * (1.0 + g * (1.0 - s))
            hid[rows(i), :] = h

            @pl.loop(0, 8)
            def _(n):
                cols = pl.ds(pl.multiple_of(n * 512, 512), 512)
                ps[z, :, :, :, cols] = dot(h, wd[:, cols]).astype(BF16).reshape(2, 2, 4, SLOT, 512)

    def backward():
        @pl.loop(0, 2)
        def _(i):
            d = dot(us[pl.ds(i * 2, 2)].reshape(256, D), wd[...], 1, 1)
            dgu[rows(i), 0:FF] = (d * fac[rows(i), :]).astype(BF16)
            dgu[rows(i), FF : 2 * FF] = (d * act[rows(i), :]).astype(BF16)

    def row_grads():
        @pl.loop(0, 2)
        def _(i):
            dg, du = dgu[rows(i), 0:FF], dgu[rows(i), FF : 2 * FF]

            @pl.loop(0, 8)
            def _(n):
                cols = pl.ds(pl.multiple_of(n * 512, 512), 512)
                g = dot(dg, wg[cols, :], 1, 1) + dot(du, wu[cols, :], 1, 1)
                qs[pl.ds(i * 2, 2), :, :, :, cols] = g.astype(BF16).reshape(2, 2, 4, SLOT, 512)

    def grad_in():
        @pl.loop(0, 8)
        def _(n):
            cols = pl.ds(pl.multiple_of(n * 512, 512), 512)
            g = dot(xs[:, :, :, :, cols].reshape(512, 512), dgu[...], 0, 0)
            gg[cols, :] = g[:, 0:FF].astype(BF16)
            gu[cols, :] = g[:, FF : 2 * FF].astype(BF16)

        return [fetch(gg, gg_hbm.at[0], 5), fetch(gu, gu_hbm.at[0], 6)]

    def grad_out():
        @pl.loop(0, 8)
        def _(n):
            cols = pl.ds(pl.multiple_of(n * 512, 512), 512)
            gd[:, cols] = dot(hid[...], us[:, :, :, :, cols].reshape(512, 512), 0, 0).astype(BF16)

        return [fetch(gd, gd_hbm.at[0], 7)]

    def send_back(n, buf):
        r = lax.broadcasted_iota(jnp.int32, (64, 16), 0)
        s = lax.broadcasted_iota(jnp.int32, (64, 16), 1)
        total = 0.0
        for q in range(4):
            turn = jnp.where((s == (r // 16) * 4 + r % 4) & ((r // 4) % 4 == q), 1.0, 0.0).astype(BF16)
            total += dot(turn, buf[own["z"], own["y"], own["x"], :, q * QUARTER : (q + 1) * QUARTER])
        box_s[n] = total.astype(BF16).reshape(4, 16, QUARTER)
        return trade(n)

    col = lax.broadcasted_iota(jnp.int32, (TOK, 64), 1)
    c_expert, c_quarter, c_spot = (col // 16).astype(F32), (col // 4) % 4, (col % 4).astype(F32)
    two = [jnp.where(jnp.broadcast_to(ids[:, k : k + 1], (TOK, 64)) == c_expert, 1.0, 0.0) for k in range(2)]
    c_earlier = dot(jnp.where(t1 < t0, 1.0, 0.0).astype(BF16), (two[0] + two[1]).astype(BF16))
    two = [jnp.where(c_earlier == c_spot, m, 0.0) for m in two]

    def spread(m, q, n):
        return dot(jnp.where(c_quarter == q, m, 0.0).astype(BF16), box_r[n].reshape(64, QUARTER))

    settle(trade_x, 0, xs)
    xw = [gather(part, xs) for part in PARTS]
    go(xw)
    settle(trade_u, 1, us)
    uw = [gather(part, us) for part in PARTS]
    go(uw)
    go(xw)
    go(xw)
    go(uw)
    go(xw)
    go(uw)
    go(xw, (2, 3, 0, 1))
    go(uw)
    go(xw)
    go(uw, (2, 3))
    for copy in get_w:
        copy.wait()
    forward()
    pw = [scatter(part, ps) for part in PARTS]
    go(uw, (0, 1))
    go(pw)
    go(uw)
    backward()
    go(pw)
    row_grads()
    qw = [scatter(part, qs) for part in PARTS]
    go(qw)
    go(pw)
    go(pw)
    go(qw)
    go(pw)
    outs = grad_in()
    go(qw)
    go(pw)
    trade_m = send_back(2, ps)
    outs += grad_out()
    go(qw)
    for copy in trade_m:
        copy.wait_recv()
    for q in range(4):
        cols = slice(q * QUARTER, (q + 1) * QUARTER)
        out_m[:, cols] = (wts[:, 0:1] * spread(two[0], q, 2) + wts[:, 1:2] * spread(two[1], q, 2)).astype(BF16)
    outs.append(fetch(out_m, mixed_hbm, 8))
    go(qw)
    go(qw)
    trade_g = send_back(3, qs)
    for copy in trade_g:
        copy.wait_recv()
    for q in range(4):
        cols = slice(q * QUARTER, (q + 1) * QUARTER)
        out_g[:, cols] = spread(two[0] + two[1], q, 3).astype(BF16)
    outs.append(fetch(out_g, gtok_hbm, 9))
    for copy in sent:
        copy.wait_send()
    for copy in outs:
        copy.wait()


def landings(part):
    width, shapes = part[1] - part[0], []
    for axis, free, halved in reversed(list(stages(part))):
        whole = tuple(SIZES[a] if a in free else 1 for a in "zyx")
        if SIZES[axis] == 2:
            shapes.append((*whole, SLOT, width))
            continue
        cut = tuple(n // 2 if a == halved else n for a, n in zip("zyx", whole))
        widths = (384, width - 384) if halved is None else (width, width)
        shapes += [(*cut, SLOT, w) for w in widths] + [(*whole, SLOT, width)] * 2
    return shapes


def local(tokens, expert_ids, route_weights, w_gate, w_up, w_down, cotangent):
    vm = lambda *shape, dtype=BF16: pltpu.VMEM(shape, dtype)
    grid5 = (4, 2, 4, SLOT, D)
    scratch = [
        vm(TOK, D), vm(TOK, D), vm(D, FF), vm(D, FF), vm(FF, D),
        vm(*grid5), vm(*grid5), vm(*grid5), vm(*grid5),
        vm(512, FF, dtype=F32), vm(512, FF, dtype=F32), vm(512, FF), vm(512, 2 * FF),
        vm(D, FF), vm(D, FF), vm(FF, D), vm(TOK, D), vm(TOK, D),
        vm(4, 4, 16, QUARTER), vm(4, 4, 16, QUARTER),
        pltpu.SemaphoreType.DMA((10,)),
        pltpu.SemaphoreType.DMA((COPIES,)),
        pltpu.SemaphoreType.DMA((COPIES,)),
    ]
    scratch += [vm(*s) for _ in range(2) for part in PARTS for s in landings(part)]
    any_spec = pl.BlockSpec(memory_space=pl.ANY)
    vmem_spec = pl.BlockSpec(memory_space=pltpu.VMEM)
    shape = jax.ShapeDtypeStruct
    return pl.pallas_call(
        kernel,
        out_shape=(
            shape((TOK, D), BF16), shape((TOK, D), BF16),
            shape((1, D, FF), BF16), shape((1, D, FF), BF16), shape((1, FF, D), BF16),
        ),
        in_specs=[vmem_spec] * 2 + [any_spec] * 5,
        out_specs=(any_spec,) * 5,
        scratch_shapes=scratch,
        compiler_params=pltpu.CompilerParams(
            collective_id=0, has_side_effects=True, vmem_limit_bytes=60 << 20
        ),
        cost_estimate=pl.CostEstimate(
            flops=9 * 2 * 512 * D * FF, bytes_accessed=16 << 20, transcendentals=512 * FF
        ),
        name="moe",
    )(expert_ids, route_weights, tokens, cotangent, w_gate, w_up, w_down)


def solution(mesh):
    rows, up, down = P(("ep", "rep"), None), P("rep", None, "ep"), P("rep", "ep", None)
    return jax.shard_map(
        local,
        mesh=mesh,
        in_specs=(rows, rows, rows, up, up, down, rows),
        out_specs=(rows, rows, up, up, down),
        check_vma=False,
    )
```

```python
import functools

import jax
import jax.numpy as jnp
from jax import lax
from jax.experimental import pallas as pl
from jax.experimental.pallas import tpu as pltpu
from jax.sharding import PartitionSpec as P

MESH = pl.DeviceIdType.MESH
F32, BF16 = jnp.float32, jnp.bfloat16
D, FF, TOK, SLOT = 4096, 256, 128, 16
QUARTER = D // 4
SIZES = {"z": 4, "y": 2, "x": 4}
PARTS = (
    (0, 1408, "yzx"),
    (1408, 2816, "yxz"),
    (2816, 3456, "zxy"),
    (3456, 4096, "xzy"),
)
LATE, CUT = 640, 384
COPIES = 340


def dot(a, b, ca=1, cb=0):
    return lax.dot_general(a, b, (((ca,), (cb,)), ((), ())), preferred_element_type=F32)


def kernel(
    ids_ref, wts_ref, tok_hbm, cot_hbm, wg_hbm, wu_hbm, wd_hbm,
    out_m, out_g, gg, gu, gd,
    tok, cot, wg, wu, wd, xs, us, ps, qs, act, fac, hid, dgu,
    box_s, box_r, local_sem, send_sem, recv_sem, *landing,
):
    ep, rep = lax.axis_index("ep"), lax.axis_index("rep")
    own = {"z": ep // 8, "y": (ep // 4) % 2, "x": ep % 4}
    half, core = rep // 2, rep % 2

    def place(z=None, y=None, x=None, h=None, c=None):
        z, y, x = (own[k] if v is None else v for k, v in (("z", z), ("y", y), ("x", x)))
        return (z * 8 + y * 4 + x, (half if h is None else h) * 2 + (core if c is None else c))

    after = {a: (own[a] + 1) % SIZES[a] for a in SIZES}
    before = {a: (own[a] + SIZES[a] - 1) % SIZES[a] for a in SIZES}
    far = {a: (own[a] + 2) % SIZES[a] for a in SIZES}

    def fetch(src, dst, i):
        copy = pltpu.make_async_copy(src, dst, local_sem.at[i])
        copy.start()
        return copy

    get_tok = fetch(tok_hbm, tok, 0)
    get_cot = fetch(cot_hbm, cot, 1)
    get_w = [fetch(wg_hbm.at[0], wg, 2), fetch(wu_hbm.at[0], wu, 3), fetch(wd_hbm.at[0], wd, 4)]

    traders = [place(c=1 - core), place(y=1 - own["y"], h=1 - half), place(y=1 - own["y"], h=1 - half, c=1 - core)]
    neighbours = traders + [place(y=1 - own["y"])]
    for a in "zx":
        neighbours += [place(**{a: after[a]}), place(**{a: before[a]})]
    barrier = pltpu.get_barrier_semaphore()
    for device in neighbours:
        pl.semaphore_signal(barrier, inc=1, device_id=device, device_id_type=MESH)

    sent = []

    def send(src, dst, device):
        i = len(sent)
        copy = pltpu.make_async_remote_copy(
            src, dst, send_sem.at[i], recv_sem.at[i], device_id=device, device_id_type=MESH
        )
        copy.start()
        sent.append(copy)
        return copy

    ids = [jnp.broadcast_to(ids_ref[k : k + 1, :].astype(F32), (TOK, TOK)) for k in range(2)]
    wts = [jnp.broadcast_to(wts_ref[k : k + 1, :], (TOK, TOK)) for k in range(2)]
    along, w_along = [a[:64] for a in ids], [w[:64] for w in wts]
    row = lax.broadcasted_iota(jnp.int32, (64, TOK), 0)
    expert, quarter, spot = row // 16, (row // 4) % 4, (row % 4).astype(F32)
    one = [jnp.where(a == expert.astype(F32), 1.0, 0.0).astype(F32) for a in along]
    hit = one[0] + one[1]
    t0 = lax.broadcasted_iota(jnp.int32, (TOK, TOK), 0)
    t1 = lax.broadcasted_iota(jnp.int32, (TOK, TOK), 1)
    earlier = dot(hit.astype(BF16), jnp.where(t0 < t1, 1.0, 0.0).astype(BF16))
    taken = jnp.where(earlier == spot, hit, 0.0)
    row_weight = jnp.sum(taken * (one[0] * w_along[0] + one[1] * w_along[1]), axis=1, keepdims=True)
    pick = [jnp.where(quarter == q, taken, 0.0).astype(BF16) for q in range(4)]

    def pack(values):
        return sum(dot(pick[q], values[:, q * QUARTER : (q + 1) * QUARTER]) for q in range(4))

    def trade(n):
        copies = [send(box_s.at[n, d[1]], box_r.at[n, rep], d) for d in traders]
        box_r[n, rep] = box_s[n, rep]
        return copies

    get_tok.wait()
    box_s[0] = pack(tok[...]).astype(BF16).reshape(4, 16, QUARTER)
    pl.semaphore_wait(barrier, len(neighbours))
    trade_x = trade(0)
    get_cot.wait()
    box_s[1] = (pack(cot[...]) * row_weight).astype(BF16).reshape(4, 16, QUARTER)
    trade_u = trade(1)

    def settle(copies, n, buf):
        for copy in copies:
            copy.wait_recv()
        r = lax.broadcasted_iota(jnp.int32, (16, 64), 0)
        s = lax.broadcasted_iota(jnp.int32, (16, 64), 1)
        blocks = box_r[n].reshape(64, QUARTER)
        for q in range(4):
            turn = jnp.where(s == (r // 4) * 16 + q * 4 + r % 4, 1.0, 0.0).astype(BF16)
            buf[own["z"], own["y"], own["x"], :, q * QUARTER : (q + 1) * QUARTER] = dot(turn, blocks).astype(BF16)

    def at(part, cut=None, **where):
        lo, hi = part[0], part[1]
        if cut is not None:
            lo, hi = (lo, lo + CUT) if cut == 0 else (lo + CUT, hi)
        index = [pl.ds(*where[a]) if a in where else pl.ds(own[a], 1) for a in "zyx"]
        return (*index, slice(None), pl.ds(lo, hi - lo))

    def all_of(axis):
        return (0, SIZES[axis])

    def sides(axis):
        return place(**{axis: after[axis]}), place(**{axis: before[axis]})

    def gather_y_first(part, buf):
        _, _, (_, a, b) = part
        (up_a, down_a), (up_b, down_b) = sides(a), sides(b)

        def push(where, device, y=(0, 2)):
            ref = buf.at[at(part, **where, y=y)]
            return send(ref, ref, device)

        def pass_on(up, down, where):
            up.wait_recv()
            up = push({**where, b: (before[b], 1)}, up_b, (0, 1))
            down.wait_recv()
            return up, push({**where, b: (after[b], 1)}, down_b, (1, 1))

        ref = buf.at[at(part)]
        y = send(ref, ref, sides("y")[0])
        yield
        y.wait_recv()
        au, ad = push({}, up_a), push({}, down_a)
        x0 = push({}, up_b), push({}, down_b)
        yield
        low, high, other = {a: (before[a], 1)}, {a: (after[a], 1)}, {a: (far[a], 1)}
        au.wait_recv()
        au = push(low, up_a, (0, 1))
        ad.wait_recv()
        ad = push(high, down_a, (1, 1))
        x1 = push(low, up_b), push(low, down_b)
        x2 = push(high, up_b), push(high, down_b)
        yield
        ends = [*pass_on(*x0, {})]
        yield
        au.wait_recv()
        ad.wait_recv()
        x3 = push(other, up_b), push(other, down_b)
        yield
        ends += [*pass_on(*x1, low), *pass_on(*x2, high)]
        yield
        ends += [*pass_on(*x3, other)]
        yield
        for copy in ends:
            copy.wait_recv()

    def gather_y_last(part, buf):
        _, _, (a, b, _) = part
        (up_a, down_a), (up_b, down_b) = sides(a), sides(b)
        over = sides("y")[0]

        def push(where, device, cut=None):
            ref = buf.at[at(part, cut, **where)]
            return send(ref, ref, device)

        au, ad = push({}, up_a), push({}, down_a)
        yield
        au.wait_recv()
        au = push({a: (before[a], 1)}, up_a, 0)
        ad.wait_recv()
        ad = push({a: (after[a], 1)}, down_a, 1)
        yield
        au.wait_recv()
        ad.wait_recv()
        whole = {a: all_of(a)}
        bu, bd = push(whole, up_b), push(whole, down_b)
        ends = [push(whole, over)]
        yield
        bu.wait_recv()
        bu = push({a: (0, 2), b: (before[b], 1)}, up_b)
        bd.wait_recv()
        bd = push({a: (2, 2), b: (after[b], 1)}, down_b)
        ends += [push({**whole, b: (before[b], 1)}, over), push({**whole, b: (after[b], 1)}, over)]
        yield
        bu.wait_recv()
        bd.wait_recv()
        ends += [push({**whole, b: (far[b], 1)}, over)]
        yield
        for copy in ends:
            copy.wait_recv()

    def gather(part, buf):
        return (gather_y_first if part[2][0] == "y" else gather_y_last)(part, buf)

    def add(buf, index, *landed):
        total = buf[index].astype(F32)
        for ref in landed:
            total += ref[...].astype(F32)
        buf[index] = total.astype(BF16)

    landing = list(landing)

    class Ring:
        def __init__(self, part, buf, axis, split, where):
            self.up, self.down = sides(axis)
            self.axis, self.buf, self.where = axis, buf, where
            self.via = [landing.pop(0) for _ in range(2)]
            self.land = [landing.pop(0) for _ in range(2)]
            self.half = [(lambda p, i=i: at(part, **{**where, axis: (p, 1)}, **split(i)[0])) for i in range(2)]
            self.part_of = [split(i)[1] for i in range(2)]

        def far(self):
            p = far[self.axis]
            self.o0 = send(self.buf.at[self.half[0](p)], self.via[0], self.up)
            self.o1 = send(self.buf.at[self.half[1](p)], self.via[1], self.down)

        def near_up(self):
            ref = self.buf.at[self.half[1](after[self.axis])]
            self.e1 = send(ref, self.land[0].at[self.part_of[1]], self.up)

        def near_down(self):
            ref = self.buf.at[self.half[0](before[self.axis])]
            self.e0 = send(ref, self.land[1].at[self.part_of[0]], self.down)

        def start(self):
            self.far()
            self.near_up()
            self.near_down()

        def middle(self):
            self.o0.wait_recv()
            index = self.half[0](after[self.axis])
            add(self.buf, index, self.via[0])
            self.f0 = send(self.buf.at[index], self.land[0].at[self.part_of[0]], self.up)
            self.o1.wait_recv()
            index = self.half[1](before[self.axis])
            add(self.buf, index, self.via[1])
            self.f1 = send(self.buf.at[index], self.land[1].at[self.part_of[1]], self.down)

        def end(self, index):
            for copy in (self.e1, self.e0, self.f0, self.f1):
                copy.wait_recv()
            add(self.buf, index, *self.land)

    def by_y(i):
        return {"y": (i, 1)}, (slice(None), pl.ds(i, 1))

    def by_columns(i):
        return {"cut": i}, (slice(None),) * 4 + ((pl.ds(0, CUT), pl.ds(CUT, LATE - CUT))[i],)

    def by_place(axis):
        def split(i):
            here = pl.ds(2 * i, 2)
            return {axis: (2 * i, 2)}, (here,) if axis == "z" else (slice(None), slice(None), here)

        return split

    def scatter_y_last(part, buf):
        _, _, (_, a, b) = part
        spots = {"far": (far[a], 1), "low": (before[a], 1), "high": (after[a], 1), "own": (own[a], 1)}
        rings = {k: Ring(part, buf, b, by_y, {a: spots[k]}) for k in ("far", "low", "high", "own")}
        last = Ring(part, buf, a, by_y, {})
        land_y = landing.pop(0)

        def finish(k):
            rings[k].end(at(part, **{a: spots[k]}, y=(0, 2)))

        def walk():
            rings["far"].start()
            rings["low"].start()
            yield
            rings["far"].middle()
            rings["high"].start()
            yield
            rings["low"].middle()
            finish("far")
            last.far()
            rings["own"].start()
            yield
            rings["high"].middle()
            finish("low")
            last.near_down()
            yield
            rings["own"].middle()
            finish("high")
            last.near_up()
            last.middle()
            yield
            finish("own")
            last.end(at(part, y=(0, 2)))
            y = send(buf.at[at(part, y=(after["y"], 1))], land_y, sides("y")[0])
            yield
            y.wait_recv()
            add(buf, at(part), land_y)

        return walk()

    def scatter_y_first(part, buf):
        _, _, (a, b, _) = part
        whole = {a: all_of(a)}
        spots = [{**whole, b: (p[b], 1)} for p in (far, before, after, own)]
        land_y = [landing.pop(0) for _ in spots]
        ring = Ring(part, buf, b, by_place(a), {})
        last = Ring(part, buf, a, by_columns, {})

        def walk():
            copies = [
                send(buf.at[at(part, **spot, y=(after["y"], 1))], land, sides("y")[0])
                for spot, land in zip(spots, land_y)
            ]

            def take(i):
                copies[i].wait_recv()
                add(buf, at(part, **spots[i]), land_y[i])

            yield
            take(0)
            ring.far()
            yield
            take(1)
            take(2)
            ring.near_down()
            ring.near_up()
            yield
            take(3)
            ring.middle()
            yield
            ring.end(at(part, **whole))
            last.start()
            yield
            last.middle()
            yield
            last.end(at(part))

        return walk()

    def scatter(part, buf):
        return (scatter_y_last if part[2][0] == "y" else scatter_y_first)(part, buf)

    def go(walks, which=(0, 1, 2, 3)):
        for w in which:
            next(walks[w], None)

    def rows(i):
        return pl.ds(i * 256, 256)

    def forward(i):
        z = pl.ds(i * 2, 2)
        x = xs[z].reshape(256, D)
        g = dot(x, wg[...])
        u = dot(x, wu[...])
        s = 1.0 / (1.0 + jnp.exp(-g))
        a = g * s
        h = (a * u).astype(BF16)
        act[rows(i), :] = a
        fac[rows(i), :] = u * s * (1.0 + g * (1.0 - s))
        hid[rows(i), :] = h

        @pl.loop(0, 8)
        def _(n):
            cols = pl.ds(pl.multiple_of(n * 512, 512), 512)
            ps[z, :, :, :, cols] = dot(h, wd[:, cols]).astype(BF16).reshape(2, 2, 4, SLOT, 512)

    def backward(i):
        d = dot(us[pl.ds(i * 2, 2)].reshape(256, D), wd[...], 1, 1)
        dgu[rows(i), 0:FF] = (d * fac[rows(i), :]).astype(BF16)
        dgu[rows(i), FF : 2 * FF] = (d * act[rows(i), :]).astype(BF16)

    def row_grads(i):
        dg, du = dgu[rows(i), 0:FF], dgu[rows(i), FF : 2 * FF]

        @pl.loop(0, 8)
        def _(n):
            cols = pl.ds(pl.multiple_of(n * 512, 512), 512)
            g = dot(dg, wg[cols, :], 1, 1) + dot(du, wu[cols, :], 1, 1)
            qs[pl.ds(i * 2, 2), :, :, :, cols] = g.astype(BF16).reshape(2, 2, 4, SLOT, 512)

    def grad_in(i):
        @pl.loop(4 * i, 4 * i + 4)
        def _(n):
            cols = pl.ds(pl.multiple_of(n * 512, 512), 512)
            g = dot(xs[:, :, :, :, cols].reshape(512, 512), dgu[...], 0, 0)
            gg[cols, :] = g[:, 0:FF].astype(BF16)
            gu[cols, :] = g[:, FF : 2 * FF].astype(BF16)

    def grad_out():
        @pl.loop(0, 8)
        def _(n):
            cols = pl.ds(pl.multiple_of(n * 512, 512), 512)
            gd[:, cols] = dot(hid[...], us[:, :, :, :, cols].reshape(512, 512), 0, 0).astype(BF16)

    def send_back(n, buf):
        r = lax.broadcasted_iota(jnp.int32, (64, 16), 0)
        s = lax.broadcasted_iota(jnp.int32, (64, 16), 1)
        total = 0.0
        for q in range(4):
            turn = jnp.where((s == (r // 16) * 4 + r % 4) & ((r // 4) % 4 == q), 1.0, 0.0).astype(BF16)
            total += dot(turn, buf[own["z"], own["y"], own["x"], :, q * QUARTER : (q + 1) * QUARTER])
        box_s[n] = total.astype(BF16).reshape(4, 16, QUARTER)
        return trade(n)

    col = lax.broadcasted_iota(jnp.int32, (TOK, 64), 1)
    c_expert, c_quarter, c_spot = (col // 16).astype(F32), (col // 4) % 4, (col % 4).astype(F32)
    two = [jnp.where(ids[k].T[:, :64] == c_expert, 1.0, 0.0) for k in range(2)]
    weight = [wts[k].T[:, 0:1] for k in range(2)]
    c_earlier = dot(jnp.where(t1 < t0, 1.0, 0.0).astype(BF16), (two[0] + two[1]).astype(BF16))
    two = [jnp.where(c_earlier == c_spot, m, 0.0) for m in two]

    def spread(m, q, n):
        return dot(jnp.where(c_quarter == q, m, 0.0).astype(BF16), box_r[n].reshape(64, QUARTER))

    settle(trade_x, 0, xs)
    xw = [gather(part, xs) for part in PARTS]
    go(xw)
    settle(trade_u, 1, us)
    uw = [gather(part, us) for part in PARTS]
    go(uw)
    go(xw)
    go(xw)
    go(uw)
    go(xw)
    go(xw)
    go(uw)
    go(xw)
    go(uw)
    go(xw)
    go(uw)
    go(xw)
    for copy in get_w:
        copy.wait()
    forward(0)
    go(uw)
    forward(1)
    go(uw)
    pw = [scatter(part, ps) for part in PARTS]
    qw = [scatter(part, qs) for part in PARTS]
    go(pw)
    go(uw)
    go(pw)
    backward(0)
    go(pw)
    backward(1)
    go(pw)
    row_grads(0)
    go(pw)
    row_grads(1)
    go(qw)
    go(pw)
    go(qw)
    grad_in(0)
    go(pw)
    trade_m = send_back(2, ps)
    go(qw)
    grad_in(1)
    go(qw)
    grad_out()
    go(qw)
    for copy in trade_m:
        copy.wait_recv()
    for q in range(4):
        cols = slice(q * QUARTER, (q + 1) * QUARTER)
        out_m[:, cols] = (weight[0] * spread(two[0], q, 2) + weight[1] * spread(two[1], q, 2)).astype(BF16)
    go(qw)
    go(qw)
    trade_g = send_back(3, qs)
    for copy in trade_g:
        copy.wait_recv()
    for q in range(4):
        cols = slice(q * QUARTER, (q + 1) * QUARTER)
        out_g[:, cols] = spread(two[0] + two[1], q, 3).astype(BF16)
    for copy in sent:
        copy.wait_send()


def landings(part):
    width, order = part[1] - part[0], part[2]

    def shape(cols=width, **sizes):
        return (*(sizes.get(a, 1) for a in "zyx"), SLOT, cols)

    if order[0] == "y":
        ring = [shape()] * 2 + [shape(y=2)] * 2
        return ring * 5 + [shape()]
    a = order[0]
    whole, cut = shape(**{a: 4}), shape(**{a: 2})
    return [whole] * 4 + [cut] * 2 + [whole] * 2 + [shape(CUT), shape(width - CUT)] + [shape()] * 2


def write_out(*refs):
    held, outs, sem = refs[:5], refs[5:10], refs[10]
    copies = [
        pltpu.make_async_copy(h, o if h.shape == o.shape else o.at[0], sem.at[i])
        for i, (h, o) in enumerate(zip(held, outs))
    ]
    for copy in copies:
        copy.start()
    for copy in copies:
        copy.wait()


def local(tokens, expert_ids, route_weights, w_gate, w_up, w_down, cotangent):
    vm = lambda *shape, dtype=BF16: pltpu.VMEM(shape, dtype)
    grid5 = (4, 2, 4, SLOT, D)
    scratch = [
        vm(TOK, D), vm(TOK, D), vm(D, FF), vm(D, FF), vm(FF, D),
        vm(*grid5), vm(*grid5), vm(*grid5), vm(*grid5),
        vm(512, FF, dtype=F32), vm(512, FF, dtype=F32), vm(512, FF), vm(512, 2 * FF),
        vm(4, 4, 16, QUARTER), vm(4, 4, 16, QUARTER),
        pltpu.SemaphoreType.DMA((5,)),
        pltpu.SemaphoreType.DMA((COPIES,)),
        pltpu.SemaphoreType.DMA((COPIES,)),
    ]
    scratch += [vm(*s) for _ in range(2) for part in PARTS for s in landings(part)]
    any_spec = pl.BlockSpec(memory_space=pl.ANY)
    vmem_spec = pl.BlockSpec(memory_space=pltpu.VMEM)
    shape = jax.ShapeDtypeStruct
    held = pl.pallas_call(
        kernel,
        out_shape=(
            vm(TOK, D), vm(TOK, D), vm(D, FF), vm(D, FF), vm(FF, D),
        ),
        in_specs=[vmem_spec] * 2 + [any_spec] * 5,
        out_specs=(vmem_spec,) * 5,
        scratch_shapes=scratch,
        compiler_params=pltpu.CompilerParams(
            collective_id=0, has_side_effects=True, vmem_limit_bytes=50 << 20
        ),
        cost_estimate=pl.CostEstimate(
            flops=9 * 2 * 512 * D * FF, bytes_accessed=16 << 20, transcendentals=512 * FF
        ),
        name="moe",
    )(expert_ids.T, route_weights.T, tokens, cotangent, w_gate, w_up, w_down)
    return pl.pallas_call(
        write_out,
        out_shape=(
            shape((TOK, D), BF16), shape((TOK, D), BF16),
            shape((1, D, FF), BF16), shape((1, D, FF), BF16), shape((1, FF, D), BF16),
        ),
        in_specs=[vmem_spec] * 5,
        out_specs=(any_spec,) * 5,
        scratch_shapes=[pltpu.SemaphoreType.DMA((5,))],
        compiler_params=pltpu.CompilerParams(vmem_limit_bytes=1 << 20),
        name="write_out",
    )(*(pltpu.with_memory_space_constraint(h, pltpu.VMEM) for h in held))


def solution(mesh):
    rows, up, down = P(("ep", "rep"), None), P("rep", None, "ep"), P("rep", "ep", None)
    return jax.shard_map(
        local,
        mesh=mesh,
        in_specs=(rows, rows, rows, up, up, down, rows),
        out_specs=(rows, rows, up, up, down),
        check_vma=False,
    )
```

```python
import math

import jax
import jax.numpy as jnp
from jax import lax
from jax.experimental import pallas as pl
from jax.experimental.pallas import tpu as pltpu
from jax.sharding import PartitionSpec as P

MESH = pl.DeviceIdType.MESH
F32, BF16 = jnp.float32, jnp.bfloat16
D, FF, TOK, SLOT = 4096, 256, 128, 16
QUARTER = D // 4
SIZES = {"z": 4, "y": 2, "x": 4}
PARTS = (
    (0, 1536, "yzx"),
    (1536, 3072, "yxz"),
    (3072, 3584, "zxy"),
    (3584, 4096, "xzy"),
)
LATE, CUT = 512, 256
ARRIVALS, DEPARTURES = 148, 20


def dot(a, b, ca=1, cb=0):
    return lax.dot_general(a, b, (((ca,), (cb,)), ((), ())), preferred_element_type=F32)


def kernel(
    ids_ref, wts_ref, tok_hbm, cot_hbm, wg_hbm, wu_hbm, wd_hbm,
    out_m, out_g, gg, gu, gd,
    tok, cot, wg, wu, wd, xs, us, ps, qs, act, fac, hid, dgu,
    box_s, box_r, local_sem, send_sem, recv_sem, *landing,
):
    ep, rep = lax.axis_index("ep"), lax.axis_index("rep")
    own = {"z": ep // 8, "y": (ep // 4) % 2, "x": ep % 4}
    half, core = rep // 2, rep % 2

    def place(z=None, y=None, x=None, h=None, c=None):
        z, y, x = (own[k] if v is None else v for k, v in (("z", z), ("y", y), ("x", x)))
        return (z * 8 + y * 4 + x, (half if h is None else h) * 2 + (core if c is None else c))

    after = {a: (own[a] + 1) % SIZES[a] for a in SIZES}
    before = {a: (own[a] + SIZES[a] - 1) % SIZES[a] for a in SIZES}
    far = {a: (own[a] + 2) % SIZES[a] for a in SIZES}

    def fetch(src, dst, i):
        copy = pltpu.make_async_copy(src, dst, local_sem.at[i])
        copy.start()
        return copy

    get_tok = fetch(tok_hbm, tok, 0)
    get_cot = fetch(cot_hbm, cot, 1)

    traders = [place(c=1 - core), place(y=1 - own["y"], h=1 - half), place(y=1 - own["y"], h=1 - half, c=1 - core)]
    neighbours = traders + [place(y=1 - own["y"])]
    for a in "zx":
        neighbours += [place(**{a: after[a]}), place(**{a: before[a]})]
    barrier = pltpu.get_barrier_semaphore()
    for device in neighbours:
        pl.semaphore_signal(barrier, inc=1, device_id=device, device_id_type=MESH)

    class Group:
        def __init__(self, sems, members):
            self.sem, self.size = sems.at[len(members)], 0
            members.append(self)

        def wait(self):
            span = wg.at[pl.ds(0, self.size // (2 * FF))]
            pltpu.make_async_copy(span, span, self.sem).wait()

    arrivals, departures = [], []

    def incoming():
        return Group(recv_sem, arrivals)

    def outgoing():
        return Group(send_sem, departures)

    def send(src, dst, device, out, into):
        pltpu.make_async_remote_copy(
            src, dst, out.sem, into.sem, device_id=device, device_id_type=MESH
        ).start()
        size = 2 * math.prod(src.shape)
        out.size += size
        into.size += size

    ids = [jnp.broadcast_to(ids_ref[k : k + 1, :].astype(F32), (TOK, TOK)) for k in range(2)]
    wts = [jnp.broadcast_to(wts_ref[k : k + 1, :], (TOK, TOK)) for k in range(2)]
    along, w_along = [a[:64] for a in ids], [w[:64] for w in wts]
    row = lax.broadcasted_iota(jnp.int32, (64, TOK), 0)
    expert, quarter, spot = row // 16, (row // 4) % 4, (row % 4).astype(F32)
    one = [jnp.where(a == expert.astype(F32), 1.0, 0.0).astype(F32) for a in along]
    hit = one[0] + one[1]
    t0 = lax.broadcasted_iota(jnp.int32, (TOK, TOK), 0)
    t1 = lax.broadcasted_iota(jnp.int32, (TOK, TOK), 1)
    earlier = dot(hit.astype(BF16), jnp.where(t0 < t1, 1.0, 0.0).astype(BF16))
    taken = jnp.where(earlier == spot, hit, 0.0)
    row_weight = jnp.sum(taken * (one[0] * w_along[0] + one[1] * w_along[1]), axis=1, keepdims=True)
    pick = [jnp.where(quarter == q, taken, 0.0).astype(BF16) for q in range(4)]

    def pack(values):
        return sum(dot(pick[q], values[:, q * QUARTER : (q + 1) * QUARTER]) for q in range(4))

    def trade(n):
        out, into = outgoing(), incoming()
        for d in traders:
            send(box_s.at[n, d[1]], box_r.at[n, rep], d, out, into)
        box_r[n, rep] = box_s[n, rep]
        return into

    get_tok.wait()
    box_s[0] = pack(tok[...]).astype(BF16).reshape(4, 16, QUARTER)
    pl.semaphore_wait(barrier, len(neighbours))
    trade_x = trade(0)
    get_cot.wait()
    get_w = [fetch(wg_hbm.at[0], wg, 2), fetch(wu_hbm.at[0], wu, 3), fetch(wd_hbm.at[0], wd, 4)]
    box_s[1] = (pack(cot[...]) * row_weight).astype(BF16).reshape(4, 16, QUARTER)
    trade_u = trade(1)

    def settle(into, n, buf):
        into.wait()
        r = lax.broadcasted_iota(jnp.int32, (16, 64), 0)
        s = lax.broadcasted_iota(jnp.int32, (16, 64), 1)
        blocks = box_r[n].reshape(64, QUARTER)
        for q in range(4):
            turn = jnp.where(s == (r // 4) * 16 + q * 4 + r % 4, 1.0, 0.0).astype(BF16)
            buf[own["z"], own["y"], own["x"], :, q * QUARTER : (q + 1) * QUARTER] = dot(turn, blocks).astype(BF16)

    def at(part, cut=None, **where):
        lo, hi = part[0], part[1]
        if cut is not None:
            lo, hi = (lo, lo + CUT) if cut == 0 else (lo + CUT, hi)
        index = [pl.ds(*where[a]) if a in where else pl.ds(own[a], 1) for a in "zyx"]
        return (*index, slice(None), pl.ds(lo, hi - lo))

    def all_of(axis):
        return (0, SIZES[axis])

    def sides(axis):
        return place(**{axis: after[axis]}), place(**{axis: before[axis]})

    def gather_y_first(part, buf):
        _, _, (_, a, b) = part
        (up_a, down_a), (up_b, down_b) = sides(a), sides(b)
        low, high, other = before[a], after[a], far[a]
        rows_y = [own["y"], 1 - own["y"]]
        out = outgoing()

        def push(j, device, into, pa=None, pb=None):
            where = {"y": (rows_y[j], 1)}
            if pa is not None:
                where[a] = (pa, 1)
            if pb is not None:
                where[b] = (pb, 1)
            ref = buf.at[at(part, **where)]
            send(ref, ref, device, out, into)

        def either(j, first, second):
            return jnp.where(rows_y[j] == 0, first, second)

        def onward(j, axis, up, down, into, **fixed):
            device = tuple(either(j, u, d) for u, d in zip(up, down))
            spot = either(j, before[axis], after[axis])
            push(j, device, into, **{"pa" if axis == a else "pb": spot}, **fixed)

        def both(j, into, pa=None):
            push(j, up_b, into, pa)
            push(j, down_b, into, pa)

        def begin(j):
            push(j, up_a, first_a[j])
            push(j, down_a, first_a[j])
            both(j, first_b[j])

        first_a, first_b, far_a, near, last = ([incoming(), incoming()] for _ in range(5))
        over, ends = incoming(), incoming()
        push(0, sides("y")[0], over)
        begin(0)
        yield
        over.wait()
        begin(1)
        yield
        for j in range(2):
            first_a[j].wait()
            onward(j, a, up_a, down_a, far_a[j])
            both(j, near[j], low)
            both(j, near[j], high)
            yield
        for j in range(2):
            first_b[j].wait()
            onward(j, b, up_b, down_b, ends)
        yield
        for j in range(2):
            far_a[j].wait()
            both(j, last[j], other)
        yield
        for j in range(2):
            near[j].wait()
            for p in (low, high):
                onward(j, b, up_b, down_b, ends, pa=p)
        yield
        for j in range(2):
            last[j].wait()
            onward(j, b, up_b, down_b, ends, pa=other)
        yield
        ends.wait()

    def gather_y_last(part, buf):
        _, _, (a, b, _) = part
        (up_a, down_a), (up_b, down_b) = sides(a), sides(b)
        over = sides("y")[0]
        out = outgoing()

        def push(where, device, into, cut=None):
            ref = buf.at[at(part, cut, **where)]
            send(ref, ref, device, out, into)

        first_a, far_a, first_b, far_b, ends = (incoming() for _ in range(5))
        push({}, up_a, first_a)
        push({}, down_a, first_a)
        yield
        yield
        first_a.wait()
        push({a: (before[a], 1)}, up_a, far_a, 0)
        push({a: (after[a], 1)}, down_a, far_a, 1)
        yield
        far_a.wait()
        whole = {a: all_of(a)}
        push(whole, up_b, first_b)
        push(whole, down_b, first_b)
        push(whole, over, ends)
        yield
        yield
        first_b.wait()
        push({a: (0, 2), b: (before[b], 1)}, up_b, far_b)
        push({a: (2, 2), b: (after[b], 1)}, down_b, far_b)
        push({**whole, b: (before[b], 1)}, over, ends)
        push({**whole, b: (after[b], 1)}, over, ends)
        yield
        far_b.wait()
        push({**whole, b: (far[b], 1)}, over, ends)
        yield
        yield
        ends.wait()

    def gather(part, buf):
        return (gather_y_first if part[2][0] == "y" else gather_y_last)(part, buf)

    def add(buf, index, *landed):
        total = buf[index].astype(F32)
        for ref in landed:
            total += ref[...].astype(F32)
        buf[index] = total.astype(BF16)

    landing = list(landing)

    class Ring:
        def __init__(self, part, buf, axis, split, where, out):
            self.up, self.down = sides(axis)
            self.axis, self.buf, self.out = axis, buf, out
            self.via = [landing.pop(0) for _ in range(2)]
            self.land = [landing.pop(0) for _ in range(2)]
            self.half = [(lambda p, i=i: at(part, **{**where, axis: (p, 1)}, **split(i)[0])) for i in range(2)]
            self.part_of = [split(i)[1] for i in range(2)]
            self.passing, self.landed = incoming(), incoming()

        def far(self):
            p = far[self.axis]
            send(self.buf.at[self.half[0](p)], self.via[0], self.up, self.out, self.passing)
            send(self.buf.at[self.half[1](p)], self.via[1], self.down, self.out, self.passing)

        def to_up(self, i, index):
            send(self.buf.at[index], self.land[0].at[self.part_of[i]], self.up, self.out, self.landed)

        def to_down(self, i, index):
            send(self.buf.at[index], self.land[1].at[self.part_of[i]], self.down, self.out, self.landed)

        def near_up(self):
            self.to_up(1, self.half[1](after[self.axis]))

        def near_down(self):
            self.to_down(0, self.half[0](before[self.axis]))

        def start(self):
            self.far()
            self.near_up()
            self.near_down()

        def middle(self):
            self.passing.wait()
            index = self.half[0](after[self.axis])
            add(self.buf, index, self.via[0])
            self.to_up(0, index)
            index = self.half[1](before[self.axis])
            add(self.buf, index, self.via[1])
            self.to_down(1, index)

        def end(self, index):
            self.landed.wait()
            add(self.buf, index, *self.land)

    def by_y(i):
        return {"y": (i, 1)}, (slice(None), pl.ds(i, 1))

    def by_columns(i):
        return {"cut": i}, (slice(None),) * 4 + ((pl.ds(0, CUT), pl.ds(CUT, LATE - CUT))[i],)

    def by_place(axis):
        def split(i):
            here = pl.ds(2 * i, 2)
            return {axis: (2 * i, 2)}, (here,) if axis == "z" else (slice(None), slice(None), here)

        return split

    def scatter_y_last(part, buf):
        _, _, (_, a, b) = part
        spots = {"far": (far[a], 1), "low": (before[a], 1), "high": (after[a], 1), "own": (own[a], 1)}
        out = outgoing()
        rings = {k: Ring(part, buf, b, by_y, {a: spots[k]}, out) for k in ("far", "low", "high", "own")}
        last = Ring(part, buf, a, by_y, {}, out)
        land_y, over = landing.pop(0), incoming()

        def finish(k):
            rings[k].end(at(part, **{a: spots[k]}, y=(0, 2)))

        def walk():
            for ring in rings.values():
                ring.far()
            yield
            for ring in rings.values():
                ring.middle()
                ring.near_down()
                ring.near_up()
                yield
            finish("far")
            last.far()
            yield
            finish("low")
            last.near_down()
            finish("high")
            last.near_up()
            yield
            last.middle()
            finish("own")
            yield
            last.end(at(part, y=(0, 2)))
            send(buf.at[at(part, y=(after["y"], 1))], land_y, sides("y")[0], out, over)
            yield
            over.wait()
            add(buf, at(part), land_y)

        return walk()

    def scatter_y_first(part, buf):
        _, _, (a, b, _) = part
        whole = {a: all_of(a)}
        spots = [{**whole, b: (p[b], 1)} for p in (far, before, after, own)]
        land_y = [landing.pop(0) for _ in spots]
        out, over = outgoing(), [incoming() for _ in spots]
        ring = Ring(part, buf, b, by_place(a), {}, out)
        last = Ring(part, buf, a, by_columns, {}, out)

        def walk():
            def give(*which):
                for i in which:
                    src = buf.at[at(part, **spots[i], y=(after["y"], 1))]
                    send(src, land_y[i], sides("y")[0], out, over[i])

            def take(i):
                over[i].wait()
                add(buf, at(part, **spots[i]), land_y[i])

            give(0, 1)
            yield
            give(2, 3)
            take(0)
            ring.far()
            yield
            take(1)
            ring.near_down()
            yield
            take(2)
            ring.near_up()
            yield
            take(3)
            ring.middle()
            yield
            ring.end(at(part, **whole))
            last.start()
            yield
            last.middle()
            yield
            last.end(at(part))

        return walk()

    def scatter(part, buf):
        return (scatter_y_last if part[2][0] == "y" else scatter_y_first)(part, buf)

    def go(walks, which=(0, 1, 2, 3)):
        for w in which:
            next(walks[w], None)

    def rows(i):
        return pl.ds(i * 256, 256)

    def forward(i):
        z = pl.ds(i * 2, 2)
        x = xs[z].reshape(256, D)
        g = dot(x, wg[...])
        u = dot(x, wu[...])
        s = 1.0 / (1.0 + jnp.exp(-g))
        a = g * s
        h = (a * u).astype(BF16)
        act[rows(i), :] = a
        fac[rows(i), :] = u * s * (1.0 + g * (1.0 - s))
        hid[rows(i), :] = h

        @pl.loop(0, 8)
        def _(n):
            cols = pl.ds(pl.multiple_of(n * 512, 512), 512)
            ps[z, :, :, :, cols] = dot(h, wd[:, cols]).astype(BF16).reshape(2, 2, 4, SLOT, 512)

    def backward(i):
        d = dot(us[pl.ds(i * 2, 2)].reshape(256, D), wd[...], 1, 1)
        dgu[rows(i), 0:FF] = (d * fac[rows(i), :]).astype(BF16)
        dgu[rows(i), FF : 2 * FF] = (d * act[rows(i), :]).astype(BF16)

    def row_grads(i):
        dg, du = dgu[rows(i), 0:FF], dgu[rows(i), FF : 2 * FF]

        @pl.loop(0, 8)
        def _(n):
            cols = pl.ds(pl.multiple_of(n * 512, 512), 512)
            g = dot(dg, wg[cols, :], 1, 1) + dot(du, wu[cols, :], 1, 1)
            qs[pl.ds(i * 2, 2), :, :, :, cols] = g.astype(BF16).reshape(2, 2, 4, SLOT, 512)

    def grad_in(i):
        @pl.loop(4 * i, 4 * i + 4)
        def _(n):
            cols = pl.ds(pl.multiple_of(n * 512, 512), 512)
            g = dot(xs[:, :, :, :, cols].reshape(512, 512), dgu[...], 0, 0)
            gg[cols, :] = g[:, 0:FF].astype(BF16)
            gu[cols, :] = g[:, FF : 2 * FF].astype(BF16)

    def grad_out():
        @pl.loop(0, 8)
        def _(n):
            cols = pl.ds(pl.multiple_of(n * 512, 512), 512)
            gd[:, cols] = dot(hid[...], us[:, :, :, :, cols].reshape(512, 512), 0, 0).astype(BF16)

    def send_back(n, buf):
        r = lax.broadcasted_iota(jnp.int32, (64, 16), 0)
        s = lax.broadcasted_iota(jnp.int32, (64, 16), 1)
        total = 0.0
        for q in range(4):
            turn = jnp.where((s == (r // 16) * 4 + r % 4) & ((r // 4) % 4 == q), 1.0, 0.0).astype(BF16)
            total += dot(turn, buf[own["z"], own["y"], own["x"], :, q * QUARTER : (q + 1) * QUARTER])
        box_s[n] = total.astype(BF16).reshape(4, 16, QUARTER)
        return trade(n)

    col = lax.broadcasted_iota(jnp.int32, (TOK, 64), 1)
    c_expert, c_quarter, c_spot = (col // 16).astype(F32), (col // 4) % 4, (col % 4).astype(F32)
    two = [jnp.where(ids[k].T[:, :64] == c_expert, 1.0, 0.0) for k in range(2)]
    weight = [wts[k].T[:, 0:1] for k in range(2)]
    c_earlier = dot(jnp.where(t1 < t0, 1.0, 0.0).astype(BF16), (two[0] + two[1]).astype(BF16))
    two = [jnp.where(c_earlier == c_spot, m, 0.0) for m in two]

    def spread(m, q, n):
        return dot(jnp.where(c_quarter == q, m, 0.0).astype(BF16), box_r[n].reshape(64, QUARTER))

    settle(trade_x, 0, xs)
    xw = [gather(part, xs) for part in PARTS]
    go(xw)
    settle(trade_u, 1, us)
    uw = [gather(part, us) for part in PARTS]
    go(uw)
    go(xw)
    go(uw)
    go(xw)
    go(xw)
    go(xw)
    go(uw)
    go(xw)
    go(uw)
    go(uw)
    go(xw)
    go(uw)
    go(xw)
    for copy in get_w:
        copy.wait()
    go(xw)
    forward(0)
    go(uw)
    forward(1)
    pw = [scatter(part, ps) for part in PARTS]
    qw = [scatter(part, qs) for part in PARTS]
    go(pw)
    go(uw)
    go(pw)
    go(pw)
    go(uw)
    backward(0)
    go(pw)
    go(pw)
    backward(1)
    go(pw)
    row_grads(0)
    go(pw)
    row_grads(1)
    go(qw)
    go(pw)
    go(qw)
    go(qw)
    go(pw)
    go(qw)
    go(qw)
    grad_in(0)
    go(pw)
    trade_m = send_back(2, ps)
    go(qw)
    grad_in(1)
    go(qw)
    grad_out()
    go(qw)
    trade_m.wait()
    for q in range(4):
        cols = slice(q * QUARTER, (q + 1) * QUARTER)
        out_m[:, cols] = (weight[0] * spread(two[0], q, 2) + weight[1] * spread(two[1], q, 2)).astype(BF16)
    go(qw)
    go(qw)
    trade_g = send_back(3, qs)
    trade_g.wait()
    for q in range(4):
        cols = slice(q * QUARTER, (q + 1) * QUARTER)
        out_g[:, cols] = spread(two[0] + two[1], q, 3).astype(BF16)
    for group in departures:
        group.wait()
    assert len(arrivals) == ARRIVALS and len(departures) == DEPARTURES


def landings(part):
    width, order = part[1] - part[0], part[2]

    def shape(cols=width, **sizes):
        return (*(sizes.get(a, 1) for a in "zyx"), SLOT, cols)

    if order[0] == "y":
        ring = [shape()] * 2 + [shape(y=2)] * 2
        return ring * 5 + [shape()]
    a = order[0]
    whole, cut = shape(**{a: 4}), shape(**{a: 2})
    return [whole] * 4 + [cut] * 2 + [whole] * 2 + [shape(CUT), shape(width - CUT)] + [shape()] * 2


def write_out(*refs):
    held, outs, sem = refs[:5], refs[5:10], refs[10]
    copies = [
        pltpu.make_async_copy(h, o if h.shape == o.shape else o.at[0], sem.at[i])
        for i, (h, o) in enumerate(zip(held, outs))
    ]
    for copy in copies:
        copy.start()
    for copy in copies:
        copy.wait()


def local(tokens, expert_ids, route_weights, w_gate, w_up, w_down, cotangent):
    vm = lambda *shape, dtype=BF16: pltpu.VMEM(shape, dtype)
    grid5 = (4, 2, 4, SLOT, D)
    scratch = [
        vm(TOK, D), vm(TOK, D), vm(D, FF), vm(D, FF), vm(FF, D),
        vm(*grid5), vm(*grid5), vm(*grid5), vm(*grid5),
        vm(512, FF, dtype=F32), vm(512, FF, dtype=F32), vm(512, FF), vm(512, 2 * FF),
        vm(4, 4, 16, QUARTER), vm(4, 4, 16, QUARTER),
        pltpu.SemaphoreType.DMA((5,)),
        pltpu.SemaphoreType.DMA((DEPARTURES,)),
        pltpu.SemaphoreType.DMA((ARRIVALS,)),
    ]
    scratch += [vm(*s) for _ in range(2) for part in PARTS for s in landings(part)]
    any_spec = pl.BlockSpec(memory_space=pl.ANY)
    vmem_spec = pl.BlockSpec(memory_space=pltpu.VMEM)
    shape = jax.ShapeDtypeStruct
    held = pl.pallas_call(
        kernel,
        out_shape=(
            vm(TOK, D), vm(TOK, D), vm(D, FF), vm(D, FF), vm(FF, D),
        ),
        in_specs=[vmem_spec] * 2 + [any_spec] * 5,
        out_specs=(vmem_spec,) * 5,
        scratch_shapes=scratch,
        compiler_params=pltpu.CompilerParams(
            collective_id=0, has_side_effects=True, vmem_limit_bytes=50 << 20
        ),
        cost_estimate=pl.CostEstimate(
            flops=9 * 2 * 512 * D * FF, bytes_accessed=16 << 20, transcendentals=512 * FF
        ),
        name="moe",
    )(expert_ids.T, route_weights.T, tokens, cotangent, w_gate, w_up, w_down)
    return pl.pallas_call(
        write_out,
        out_shape=(
            shape((TOK, D), BF16), shape((TOK, D), BF16),
            shape((1, D, FF), BF16), shape((1, D, FF), BF16), shape((1, FF, D), BF16),
        ),
        in_specs=[vmem_spec] * 5,
        out_specs=(any_spec,) * 5,
        scratch_shapes=[pltpu.SemaphoreType.DMA((5,))],
        compiler_params=pltpu.CompilerParams(vmem_limit_bytes=1 << 20),
        name="write_out",
    )(*(pltpu.with_memory_space_constraint(h, pltpu.VMEM) for h in held))


def solution(mesh):
    rows, up, down = P(("ep", "rep"), None), P("rep", None, "ep"), P("rep", "ep", None)
    return jax.shard_map(
        local,
        mesh=mesh,
        in_specs=(rows, rows, rows, up, up, down, rows),
        out_specs=(rows, rows, up, up, down),
        check_vma=False,
    )
```

```python
import math

import jax
import jax.numpy as jnp
from jax import lax
from jax.experimental import pallas as pl
from jax.experimental.pallas import tpu as pltpu
from jax.sharding import PartitionSpec as P

MESH = pl.DeviceIdType.MESH
F32, BF16 = jnp.float32, jnp.bfloat16
D, FF, TOK, SLOT = 4096, 256, 128, 16
QUARTER = D // 4
SIZES = {"z": 4, "y": 2, "x": 4}
PARTS = (
    (0, 1536, "yzx"),
    (1536, 3072, "yxz"),
    (3072, 3584, "zxy"),
    (3584, 4096, "xzy"),
)
LATE, CUT = 512, 256
ARRIVALS, DEPARTURES = 148, 20


def dot(a, b, ca=1, cb=0):
    return lax.dot_general(a, b, (((ca,), (cb,)), ((), ())), preferred_element_type=F32)


def kernel(
    ids_ref, wts_ref, tok_hbm, cot_hbm, wg_hbm, wu_hbm, wd_hbm,
    out_m, out_g, gg, gu, gd,
    tok, cot, wg, wu, wd, xs, us, ps, qs, act, fac, hid, dgu,
    box_s, box_r, local_sem, send_sem, recv_sem, *landing,
):
    ep, rep = lax.axis_index("ep"), lax.axis_index("rep")
    own = {"z": ep // 8, "y": (ep // 4) % 2, "x": ep % 4}
    half, core = rep // 2, rep % 2

    def place(z=None, y=None, x=None, h=None, c=None):
        z, y, x = (own[k] if v is None else v for k, v in (("z", z), ("y", y), ("x", x)))
        return (z * 8 + y * 4 + x, (half if h is None else h) * 2 + (core if c is None else c))

    after = {a: (own[a] + 1) % SIZES[a] for a in SIZES}
    before = {a: (own[a] + SIZES[a] - 1) % SIZES[a] for a in SIZES}
    far = {a: (own[a] + 2) % SIZES[a] for a in SIZES}

    def fetch(src, dst, i):
        copy = pltpu.make_async_copy(src, dst, local_sem.at[i])
        copy.start()
        return copy

    get_tok = fetch(tok_hbm, tok, 0)
    get_cot = fetch(cot_hbm, cot, 1)

    traders = [place(c=1 - core), place(y=1 - own["y"], h=1 - half), place(y=1 - own["y"], h=1 - half, c=1 - core)]
    neighbours = traders + [place(y=1 - own["y"])]
    for a in "zx":
        neighbours += [place(**{a: after[a]}), place(**{a: before[a]})]
    barrier = pltpu.get_barrier_semaphore()
    for device in neighbours:
        pl.semaphore_signal(barrier, inc=1, device_id=device, device_id_type=MESH)

    class Group:
        def __init__(self, sems, members):
            self.sem, self.size = sems.at[len(members)], 0
            members.append(self)

        def wait(self):
            span = wg.at[pl.ds(0, self.size // (2 * FF))]
            pltpu.make_async_copy(span, span, self.sem).wait()

    arrivals, departures = [], []

    def incoming():
        return Group(recv_sem, arrivals)

    def outgoing():
        return Group(send_sem, departures)

    def send(src, dst, device, out, into):
        pltpu.make_async_remote_copy(
            src, dst, out.sem, into.sem, device_id=device, device_id_type=MESH
        ).start()
        size = 2 * math.prod(src.shape)
        out.size += size
        into.size += size

    ids = [jnp.broadcast_to(ids_ref[k : k + 1, :].astype(F32), (TOK, TOK)) for k in range(2)]
    wts = [jnp.broadcast_to(wts_ref[k : k + 1, :], (TOK, TOK)) for k in range(2)]
    along, w_along = [a[:64] for a in ids], [w[:64] for w in wts]
    row = lax.broadcasted_iota(jnp.int32, (64, TOK), 0)
    expert, quarter, spot = row // 16, (row // 4) % 4, (row % 4).astype(F32)
    one = [jnp.where(a == expert.astype(F32), 1.0, 0.0).astype(F32) for a in along]
    hit = one[0] + one[1]
    t0 = lax.broadcasted_iota(jnp.int32, (TOK, TOK), 0)
    t1 = lax.broadcasted_iota(jnp.int32, (TOK, TOK), 1)
    earlier = dot(hit.astype(BF16), jnp.where(t0 < t1, 1.0, 0.0).astype(BF16))
    taken = jnp.where(earlier == spot, hit, 0.0)
    row_weight = jnp.sum(taken * (one[0] * w_along[0] + one[1] * w_along[1]), axis=1, keepdims=True)
    pick = [jnp.where(quarter == q, taken, 0.0).astype(BF16) for q in range(4)]

    def pack(values):
        return sum(dot(pick[q], values[:, q * QUARTER : (q + 1) * QUARTER]) for q in range(4))

    def trade(n):
        out, into = outgoing(), incoming()
        for d in traders:
            send(box_s.at[n, d[1]], box_r.at[n, rep], d, out, into)
        box_r[n, rep] = box_s[n, rep]
        return into

    get_tok.wait()
    box_s[0] = pack(tok[...]).astype(BF16).reshape(4, 16, QUARTER)
    pl.semaphore_wait(barrier, len(neighbours))
    trade_x = trade(0)
    get_cot.wait()
    get_w = [fetch(wg_hbm.at[0], wg, 2), fetch(wu_hbm.at[0], wu, 3), fetch(wd_hbm.at[0], wd, 4)]
    box_s[1] = (pack(cot[...]) * row_weight).astype(BF16).reshape(4, 16, QUARTER)
    trade_u = trade(1)

    def settle(into, n, buf):
        into.wait()
        r = lax.broadcasted_iota(jnp.int32, (16, 64), 0)
        s = lax.broadcasted_iota(jnp.int32, (16, 64), 1)
        blocks = box_r[n].reshape(64, QUARTER)
        for q in range(4):
            turn = jnp.where(s == (r // 4) * 16 + q * 4 + r % 4, 1.0, 0.0).astype(BF16)
            buf[own["z"], own["y"], own["x"], :, q * QUARTER : (q + 1) * QUARTER] = dot(turn, blocks).astype(BF16)

    def at(part, cut=None, **where):
        lo, hi = part[0], part[1]
        if cut is not None:
            lo, hi = (lo, lo + CUT) if cut == 0 else (lo + CUT, hi)
        index = [pl.ds(*where[a]) if a in where else pl.ds(own[a], 1) for a in "zyx"]
        return (*index, slice(None), pl.ds(lo, hi - lo))

    def all_of(axis):
        return (0, SIZES[axis])

    def sides(axis):
        return place(**{axis: after[axis]}), place(**{axis: before[axis]})

    def gather_y_first(part, buf):
        _, _, (_, a, b) = part
        (up_a, down_a), (up_b, down_b) = sides(a), sides(b)
        low, high, other = before[a], after[a], far[a]
        rows_y = [own["y"], 1 - own["y"]]
        out = outgoing()

        def push(j, device, into, pa=None, pb=None):
            where = {"y": (rows_y[j], 1)}
            if pa is not None:
                where[a] = (pa, 1)
            if pb is not None:
                where[b] = (pb, 1)
            ref = buf.at[at(part, **where)]
            send(ref, ref, device, out, into)

        def either(j, first, second):
            return jnp.where(rows_y[j] == 0, first, second)

        def onward(j, axis, up, down, into, **fixed):
            device = tuple(either(j, u, d) for u, d in zip(up, down))
            spot = either(j, before[axis], after[axis])
            push(j, device, into, **{"pa" if axis == a else "pb": spot}, **fixed)

        def both(j, into, pa=None):
            push(j, up_b, into, pa)
            push(j, down_b, into, pa)

        def begin(j):
            push(j, up_a, first_a[j])
            push(j, down_a, first_a[j])
            both(j, first_b[j])

        first_a, first_b, far_a, near, last = ([incoming(), incoming()] for _ in range(5))
        over, ends = incoming(), incoming()
        push(0, sides("y")[0], over)
        begin(0)
        yield
        over.wait()
        begin(1)
        yield
        for j in range(2):
            first_a[j].wait()
            onward(j, a, up_a, down_a, far_a[j])
            both(j, near[j], low)
            both(j, near[j], high)
            yield
        for j in range(2):
            first_b[j].wait()
            onward(j, b, up_b, down_b, ends)
        yield
        for j in range(2):
            far_a[j].wait()
            both(j, last[j], other)
        yield
        for j in range(2):
            near[j].wait()
            for p in (low, high):
                onward(j, b, up_b, down_b, ends, pa=p)
        yield
        for j in range(2):
            last[j].wait()
            onward(j, b, up_b, down_b, ends, pa=other)
        yield
        ends.wait()

    def gather_y_last(part, buf):
        _, _, (a, b, _) = part
        (up_a, down_a), (up_b, down_b) = sides(a), sides(b)
        over = sides("y")[0]
        out = outgoing()

        def push(where, device, into, cut=None):
            ref = buf.at[at(part, cut, **where)]
            send(ref, ref, device, out, into)

        first_a, far_a, first_b, far_b, ends = (incoming() for _ in range(5))
        push({}, up_a, first_a)
        push({}, down_a, first_a)
        yield
        yield
        first_a.wait()
        push({a: (before[a], 1)}, up_a, far_a, 0)
        push({a: (after[a], 1)}, down_a, far_a, 1)
        yield
        far_a.wait()
        whole = {a: all_of(a)}
        push(whole, up_b, first_b)
        push(whole, down_b, first_b)
        push(whole, over, ends)
        yield
        yield
        first_b.wait()
        push({a: (0, 2), b: (before[b], 1)}, up_b, far_b)
        push({a: (2, 2), b: (after[b], 1)}, down_b, far_b)
        push({**whole, b: (before[b], 1)}, over, ends)
        push({**whole, b: (after[b], 1)}, over, ends)
        yield
        far_b.wait()
        push({**whole, b: (far[b], 1)}, over, ends)
        yield
        yield
        ends.wait()

    def gather(part, buf):
        return (gather_y_first if part[2][0] == "y" else gather_y_last)(part, buf)

    def add(buf, index, *landed):
        total = buf[index].astype(F32)
        for ref in landed:
            total += ref[...].astype(F32)
        buf[index] = total.astype(BF16)

    landing = list(landing)

    class Ring:
        def __init__(self, part, buf, axis, split, where, out):
            self.up, self.down = sides(axis)
            self.axis, self.buf, self.out = axis, buf, out
            self.via = [landing.pop(0) for _ in range(2)]
            self.land = [landing.pop(0) for _ in range(2)]
            self.half = [(lambda p, i=i: at(part, **{**where, axis: (p, 1)}, **split(i)[0])) for i in range(2)]
            self.part_of = [split(i)[1] for i in range(2)]
            self.passing, self.landed = incoming(), incoming()

        def far(self):
            p = far[self.axis]
            send(self.buf.at[self.half[0](p)], self.via[0], self.up, self.out, self.passing)
            send(self.buf.at[self.half[1](p)], self.via[1], self.down, self.out, self.passing)

        def to_up(self, i, index):
            send(self.buf.at[index], self.land[0].at[self.part_of[i]], self.up, self.out, self.landed)

        def to_down(self, i, index):
            send(self.buf.at[index], self.land[1].at[self.part_of[i]], self.down, self.out, self.landed)

        def near_up(self):
            self.to_up(1, self.half[1](after[self.axis]))

        def near_down(self):
            self.to_down(0, self.half[0](before[self.axis]))

        def start(self):
            self.far()
            self.near_up()
            self.near_down()

        def middle(self):
            self.passing.wait()
            index = self.half[0](after[self.axis])
            add(self.buf, index, self.via[0])
            self.to_up(0, index)
            index = self.half[1](before[self.axis])
            add(self.buf, index, self.via[1])
            self.to_down(1, index)

        def end(self, index):
            self.landed.wait()
            add(self.buf, index, *self.land)

    def by_y(i):
        return {"y": (i, 1)}, (slice(None), pl.ds(i, 1))

    def by_columns(i):
        return {"cut": i}, (slice(None),) * 4 + ((pl.ds(0, CUT), pl.ds(CUT, LATE - CUT))[i],)

    def by_place(axis):
        def split(i):
            here = pl.ds(2 * i, 2)
            return {axis: (2 * i, 2)}, (here,) if axis == "z" else (slice(None), slice(None), here)

        return split

    def scatter_y_last(part, buf):
        _, _, (_, a, b) = part
        spots = {"far": (far[a], 1), "low": (before[a], 1), "high": (after[a], 1), "own": (own[a], 1)}
        out = outgoing()
        rings = {k: Ring(part, buf, b, by_y, {a: spots[k]}, out) for k in ("far", "low", "high", "own")}
        last = Ring(part, buf, a, by_y, {}, out)
        land_y, over = landing.pop(0), incoming()

        def finish(k):
            rings[k].end(at(part, **{a: spots[k]}, y=(0, 2)))

        def walk():
            for ring in rings.values():
                ring.far()
            yield
            for ring in rings.values():
                ring.middle()
                ring.near_down()
                ring.near_up()
                yield
            finish("far")
            last.far()
            yield
            finish("low")
            last.near_down()
            finish("high")
            last.near_up()
            yield
            last.middle()
            finish("own")
            yield
            last.end(at(part, y=(0, 2)))
            send(buf.at[at(part, y=(after["y"], 1))], land_y, sides("y")[0], out, over)
            yield
            over.wait()
            add(buf, at(part), land_y)

        return walk()

    def scatter_y_first(part, buf):
        _, _, (a, b, _) = part
        whole = {a: all_of(a)}
        spots = [{**whole, b: (p[b], 1)} for p in (far, before, after, own)]
        land_y = [landing.pop(0) for _ in spots]
        out, over = outgoing(), [incoming() for _ in spots]
        ring = Ring(part, buf, b, by_place(a), {}, out)
        last = Ring(part, buf, a, by_columns, {}, out)

        def walk():
            def give(*which):
                for i in which:
                    src = buf.at[at(part, **spots[i], y=(after["y"], 1))]
                    send(src, land_y[i], sides("y")[0], out, over[i])

            def take(i):
                over[i].wait()
                add(buf, at(part, **spots[i]), land_y[i])

            give(0, 1)
            yield
            give(2, 3)
            yield
            take(0)
            ring.far()
            yield
            take(1)
            ring.near_down()
            yield
            take(2)
            ring.near_up()
            yield
            take(3)
            ring.middle()
            yield
            ring.end(at(part, **whole))
            last.start()
            yield
            last.middle()
            yield
            last.end(at(part))

        return walk()

    def scatter(part, buf):
        return (scatter_y_last if part[2][0] == "y" else scatter_y_first)(part, buf)

    def go(walks, which=(0, 1, 2, 3)):
        for w in which:
            next(walks[w], None)

    def rows(i):
        return pl.ds(i * 256, 256)

    def hidden(i):
        x = xs[pl.ds(i * 2, 2)].reshape(256, D)
        g = dot(x, wg[...])
        u = dot(x, wu[...])
        s = 1.0 / (1.0 + jnp.exp(-g))
        a = g * s
        act[rows(i), :] = a
        fac[rows(i), :] = u * s * (1.0 + g * (1.0 - s))
        hid[rows(i), :] = (a * u).astype(BF16)

    def by_block(p, body):
        lo, hi, _ = PARTS[p]

        @pl.loop(lo // 512, hi // 512)
        def _(n):
            cols = pl.ds(pl.multiple_of(n * 512, 512), 512)
            for i in range(2):
                body(i, cols)

    def routed(p):
        def body(i, cols):
            r = dot(hid[rows(i), :], wd[:, cols])
            ps[pl.ds(i * 2, 2), :, :, :, cols] = r.astype(BF16).reshape(2, 2, 4, SLOT, 512)

        by_block(p, body)

    def backward(i):
        d = dot(us[pl.ds(i * 2, 2)].reshape(256, D), wd[...], 1, 1)
        dgu[rows(i), 0:FF] = (d * fac[rows(i), :]).astype(BF16)
        dgu[rows(i), FF : 2 * FF] = (d * act[rows(i), :]).astype(BF16)

    def row_grads(p):
        def body(i, cols):
            g = dot(dgu[rows(i), 0:FF], wg[cols, :], 1, 1) + dot(dgu[rows(i), FF : 2 * FF], wu[cols, :], 1, 1)
            qs[pl.ds(i * 2, 2), :, :, :, cols] = g.astype(BF16).reshape(2, 2, 4, SLOT, 512)

        by_block(p, body)

    def grad_in(i):
        @pl.loop(2 * i, 2 * i + 2)
        def _(n):
            cols = pl.ds(pl.multiple_of(n * 512, 512), 512)
            g = dot(xs[:, :, :, :, cols].reshape(512, 512), dgu[...], 0, 0)
            gg[cols, :] = g[:, 0:FF].astype(BF16)
            gu[cols, :] = g[:, FF : 2 * FF].astype(BF16)

    def grad_out(i):
        @pl.loop(4 * i, 4 * i + 4)
        def _(n):
            cols = pl.ds(pl.multiple_of(n * 512, 512), 512)
            gd[:, cols] = dot(hid[...], us[:, :, :, :, cols].reshape(512, 512), 0, 0).astype(BF16)

    def send_back(n, buf):
        r = lax.broadcasted_iota(jnp.int32, (64, 16), 0)
        s = lax.broadcasted_iota(jnp.int32, (64, 16), 1)
        total = 0.0
        for q in range(4):
            turn = jnp.where((s == (r // 16) * 4 + r % 4) & ((r // 4) % 4 == q), 1.0, 0.0).astype(BF16)
            total += dot(turn, buf[own["z"], own["y"], own["x"], :, q * QUARTER : (q + 1) * QUARTER])
        box_s[n] = total.astype(BF16).reshape(4, 16, QUARTER)
        return trade(n)

    col = lax.broadcasted_iota(jnp.int32, (TOK, 64), 1)
    c_expert, c_quarter, c_spot = (col // 16).astype(F32), (col // 4) % 4, (col % 4).astype(F32)
    two = [jnp.where(ids[k].T[:, :64] == c_expert, 1.0, 0.0) for k in range(2)]
    weight = [wts[k].T[:, 0:1] for k in range(2)]
    c_earlier = dot(jnp.where(t1 < t0, 1.0, 0.0).astype(BF16), (two[0] + two[1]).astype(BF16))
    two = [jnp.where(c_earlier == c_spot, m, 0.0) for m in two]

    def spread(m, q, n):
        return dot(jnp.where(c_quarter == q, m, 0.0).astype(BF16), box_r[n].reshape(64, QUARTER))

    settle(trade_x, 0, xs)
    xw = [gather(part, xs) for part in PARTS]
    go(xw, (0,))
    go(xw, (1,))
    go(xw, (2,))
    go(xw, (3,))
    settle(trade_u, 1, us)
    uw = [gather(part, us) for part in PARTS]
    go(xw, (3,))
    go(xw, (2,))
    go(uw, (0,))
    go(uw, (3,))
    go(uw, (3,))
    go(uw, (2,))
    go(xw, (0,))
    go(xw, (0,))
    go(uw, (2,))
    go(uw, (1,))
    go(xw, (1,))
    go(xw, (3,))
    go(xw, (2,))
    go(xw, (1,))
    go(uw, (0,))
    go(uw, (0,))
    go(uw, (3,))
    go(uw, (2,))
    go(uw, (1,))
    go(xw, (0,))
    go(xw, (0,))
    go(uw, (1,))
    go(xw, (2,))
    go(xw, (2,))
    go(xw, (1,))
    go(xw, (3,))
    go(xw, (3,))
    go(xw, (1,))
    go(uw, (0,))
    go(uw, (0,))
    go(xw, (0,))
    go(uw, (2,))
    go(uw, (2,))
    go(uw, (3,))
    go(uw, (3,))
    go(uw, (1,))
    go(uw, (1,))
    go(xw, (0,))
    go(xw, (3,))
    go(xw, (1,))
    go(xw, (1,))
    go(xw, (2,))
    go(uw, (0,))
    go(uw, (3,))
    go(uw, (0,))
    go(xw, (0,))
    go(xw, (3,))
    go(xw, (3,))
    go(uw, (2,))
    go(uw, (1,))
    go(xw, (1,))
    go(uw, (1,))
    go(xw, (2,))
    go(xw, (2,))
    go(uw, (3,))
    go(uw, (3,))
    go(xw, (3,))
    go(uw, (0,))
    go(uw, (1,))
    go(xw, (1,))
    go(xw, (0,))
    go(xw, (2,))
    for copy in get_w:
        copy.wait()
    hidden(0)
    hidden(1)
    go(uw, (0,))
    go(uw, (3,))
    go(uw, (2,))
    go(uw, (2,))
    go(uw, (1,))
    routed(1)
    pw = [scatter(part, ps) for part in PARTS]
    qw = [scatter(part, qs) for part in PARTS]
    go(pw, (1,))
    routed(0)
    go(pw, (0,))
    go(uw, (2,))
    backward(1)
    routed(2)
    go(pw, (1,))
    go(pw, (2,))
    go(pw, (2,))
    backward(0)
    go(pw, (1,))
    go(pw, (0,))
    row_grads(3)
    go(qw, (3,))
    go(qw, (3,))
    go(pw, (1,))
    go(pw, (0,))
    go(pw, (1,))
    go(pw, (2,))
    go(pw, (0,))
    row_grads(1)
    go(qw, (1,))
    go(pw, (1,))
    go(pw, (2,))
    go(pw, (2,))
    go(pw, (0,))
    go(pw, (0,))
    row_grads(2)
    go(qw, (2,))
    go(qw, (2,))
    row_grads(0)
    go(qw, (0,))
    go(qw, (3,))
    go(qw, (3,))
    go(pw, (1,))
    go(pw, (2,))
    go(pw, (0,))
    go(qw, (3,))
    go(qw, (1,))
    go(pw, (1,))
    routed(3)
    go(qw, (1,))
    go(pw, (3,))
    go(pw, (3,))
    grad_in(2)
    go(qw, (2,))
    go(qw, (1,))
    go(qw, (1,))
    go(qw, (2,))
    go(qw, (0,))
    go(pw, (0,))
    grad_out(0)
    go(qw, (0,))
    go(qw, (0,))
    go(qw, (3,))
    go(qw, (2,))
    grad_in(3)
    go(qw, (0,))
    go(pw, (3,))
    grad_out(1)
    go(qw, (1,))
    go(pw, (3,))
    go(pw, (1,))
    go(pw, (2,))
    go(qw, (2,))
    go(pw, (3,))
    grad_in(0)
    grad_in(1)
    go(qw, (0,))
    go(qw, (1,))
    go(pw, (1,))
    go(pw, (0,))
    go(qw, (3,))
    go(qw, (0,))
    go(pw, (3,))
    go(pw, (2,))
    go(pw, (0,))
    go(qw, (0,))
    go(qw, (1,))
    go(qw, (2,))
    go(pw, (3,))
    go(pw, (2,))
    go(qw, (3,))
    go(qw, (0,))
    go(qw, (2,))
    go(qw, (1,))
    go(pw, (3,))
    go(qw, (3,))
    go(qw, (2,))
    go(qw, (0,))
    go(pw, (3,))
    trade_m = send_back(2, ps)
    go(qw, (1,))
    trade_g = send_back(3, qs)
    trade_m.wait()
    for q in range(4):
        cols = slice(q * QUARTER, (q + 1) * QUARTER)
        out_m[:, cols] = (weight[0] * spread(two[0], q, 2) + weight[1] * spread(two[1], q, 2)).astype(BF16)
    trade_g.wait()
    for q in range(4):
        cols = slice(q * QUARTER, (q + 1) * QUARTER)
        out_g[:, cols] = spread(two[0] + two[1], q, 3).astype(BF16)
    for group in departures:
        group.wait()
    assert len(arrivals) == ARRIVALS and len(departures) == DEPARTURES


def landings(part):
    width, order = part[1] - part[0], part[2]

    def shape(cols=width, **sizes):
        return (*(sizes.get(a, 1) for a in "zyx"), SLOT, cols)

    if order[0] == "y":
        ring = [shape()] * 2 + [shape(y=2)] * 2
        return ring * 5 + [shape()]
    a = order[0]
    whole, cut = shape(**{a: 4}), shape(**{a: 2})
    return [whole] * 4 + [cut] * 2 + [whole] * 2 + [shape(CUT), shape(width - CUT)] + [shape()] * 2


def write_out(*refs):
    held, outs, sem = refs[:5], refs[5:10], refs[10]
    copies = [
        pltpu.make_async_copy(h, o if h.shape == o.shape else o.at[0], sem.at[i])
        for i, (h, o) in enumerate(zip(held, outs))
    ]
    for copy in copies:
        copy.start()
    for copy in copies:
        copy.wait()


def local(tokens, expert_ids, route_weights, w_gate, w_up, w_down, cotangent):
    vm = lambda *shape, dtype=BF16: pltpu.VMEM(shape, dtype)
    grid5 = (4, 2, 4, SLOT, D)
    scratch = [
        vm(TOK, D), vm(TOK, D), vm(D, FF), vm(D, FF), vm(FF, D),
        vm(*grid5), vm(*grid5), vm(*grid5), vm(*grid5),
        vm(512, FF, dtype=F32), vm(512, FF, dtype=F32), vm(512, FF), vm(512, 2 * FF),
        vm(4, 4, 16, QUARTER), vm(4, 4, 16, QUARTER),
        pltpu.SemaphoreType.DMA((5,)),
        pltpu.SemaphoreType.DMA((DEPARTURES,)),
        pltpu.SemaphoreType.DMA((ARRIVALS,)),
    ]
    scratch += [vm(*s) for _ in range(2) for part in PARTS for s in landings(part)]
    any_spec = pl.BlockSpec(memory_space=pl.ANY)
    vmem_spec = pl.BlockSpec(memory_space=pltpu.VMEM)
    shape = jax.ShapeDtypeStruct
    held = pl.pallas_call(
        kernel,
        out_shape=(
            vm(TOK, D), vm(TOK, D), vm(D, FF), vm(D, FF), vm(FF, D),
        ),
        in_specs=[vmem_spec] * 2 + [any_spec] * 5,
        out_specs=(vmem_spec,) * 5,
        scratch_shapes=scratch,
        compiler_params=pltpu.CompilerParams(
            collective_id=0, has_side_effects=True, vmem_limit_bytes=50 << 20
        ),
        cost_estimate=pl.CostEstimate(
            flops=9 * 2 * 512 * D * FF, bytes_accessed=16 << 20, transcendentals=512 * FF
        ),
        name="moe",
    )(expert_ids.T, route_weights.T, tokens, cotangent, w_gate, w_up, w_down)
    return pl.pallas_call(
        write_out,
        out_shape=(
            shape((TOK, D), BF16), shape((TOK, D), BF16),
            shape((1, D, FF), BF16), shape((1, D, FF), BF16), shape((1, FF, D), BF16),
        ),
        in_specs=[vmem_spec] * 5,
        out_specs=(any_spec,) * 5,
        scratch_shapes=[pltpu.SemaphoreType.DMA((5,))],
        compiler_params=pltpu.CompilerParams(vmem_limit_bytes=1 << 20),
        name="write_out",
    )(*(pltpu.with_memory_space_constraint(h, pltpu.VMEM) for h in held))


def solution(mesh):
    rows, up, down = P(("ep", "rep"), None), P("rep", None, "ep"), P("rep", "ep", None)
    return jax.shard_map(
        local,
        mesh=mesh,
        in_specs=(rows, rows, rows, up, up, down, rows),
        out_specs=(rows, rows, up, up, down),
        check_vma=False,
    )
```
